256 devices in a mesh: wide: 16 (over z, core), narrow: 16 (over y, x).
Axes of the slice: x: 4, y: 4, z: 8, core: 2. Of those that a mesh axis runs over, the one named last changes fastest.
Arguments:
- query_rows: bfloat16 [65536, 2048], P(('wide', 'narrow')), may hold values from -52 to 52
- key_rows: bfloat16 [65536, 512], P(('wide', 'narrow')), may hold values from -5 to 5
- value_rows: bfloat16 [65536, 512], P(('wide', 'narrow')), may hold values from -6 to 6
- doc_lengths: int32 [32], replicated, may hold values from 1 to 4096, 65536 in all
Outputs:
- attended: bfloat16 [65536, 2048], P(('wide', 'narrow'))
The draws below stay inside these ranges and needn't reach their ends.
Inputs may be any that keep to these rules, and one draw needn't show every extreme that they name: `doc_lengths`: lengths sum to 65536; the longest document has exactly 4096 tokens.
All inputs are finite; a program needn't handle non-finite values.
Results may differ from the reference program's by a relative error of at most 0.0085.
Values may be sent and summed in bfloat16 or wider, within the bound.
No kernel may reach another device: no remote copies, remote signals or barrier semaphores. Data moves between devices by JAX's collectives and lax.ppermute only.
A program may use at most 64 MiB of HBM per device.

```python
import math
import jax
import jax.numpy as jnp
import numpy as np
from jax import lax

HEADS = 16
KV_HEADS = 4
HEAD_DIM = 128
TOKENS = 65536
SECTION = 4096
DOCS = 32


def key_table(key):
    base = jax.random.fold_in(key, 11)
    table = jnp.clip(jax.random.normal(base, (TOKENS, KV_HEADS * HEAD_DIM), jnp.float32), -5.0, 5.0)
    return table


def draw_key_rows(key, part):
    return key_table(key).astype(jnp.bfloat16)


def draw_query_rows(key, part):
    fresh_key = jax.random.fold_in(key, 23)
    fresh = jnp.clip(jax.random.normal(fresh_key, (TOKENS, HEADS * HEAD_DIM), jnp.float32), -5.0, 5.0)
    return fresh.astype(jnp.bfloat16)


def steps_of(own_key, extent, cuts, smallest, high):
    loudness = 1.0
    for position, shards_of in cuts:
        heights = jax.random.uniform(jax.random.fold_in(jax.random.fold_in(own_key, 6), position), (shards_of,), jnp.float32, smallest / len(cuts), high / len(cuts))
        loudness = loudness * jnp.repeat(jnp.exp(heights), extent[position] // shards_of).reshape((-1,) + (1,) * (len(extent) - 1 - position))
    return loudness


def split_up(amount, total, reach, skew):
    weights = [(1 << 20) // math.isqrt(rank ** skew) + 1 for rank in range(2, amount + 1)]
    spare, given = total - reach - (amount - 1), [1] * (amount - 1)
    while spare > 0:
        candidates = [i for i in range(amount - 1) if given[i] < reach]
        whole, budget = sum([weights[i] for i in candidates]), spare
        for i in candidates:
            more = min(reach - given[i], max(1, budget * weights[i] // whole), spare)
            given[i] = given[i] + more
            spare = spare - more
    return np.array([reach] + given)


def uneven_parts(key, amount, total, most, lean):
    if amount == 2:
        one = jax.random.randint(key, (), max(1, total - most), min(most, total - 1) + 1)
        return jnp.stack([one, total - one])
    tallies = jnp.asarray(split_up(amount, total, most, lean), jnp.int32)
    couples = (amount - 1) // 2
    source_of, receiver = tallies[1:1 + 2 * couples:2], tallies[2:2 + 2 * couples:2]
    room = jnp.minimum(source_of - 1, most - receiver)
    passed = jax.random.randint(jax.random.fold_in(key, 1), (couples,), 0, 1 << 20) % (room + 1)
    tallies = tallies.at[1:1 + 2 * couples:2].set(source_of - passed).at[2:2 + 2 * couples:2].set(receiver + passed)
    return tallies[jax.random.permutation(jax.random.fold_in(key, 2), amount)]


def normal_values(rng, dims, width, bound, pieces=(), kind=jnp.bfloat16):
    values = jax.random.normal(rng, dims, jnp.float32) * width
    if len(pieces) > 0:
        values = steps_of(rng, dims, pieces, -0.22, 0.18) * values
    return jnp.clip(values, min=-bound, max=bound).astype(kind)


def setup_inputs(seed: int = 0) -> dict:
    key_list = jax.random.split(jax.random.key(seed), 5)
    return {
        "query_rows": draw_query_rows(jax.random.fold_in(key_list[4], 71), 0),
        "key_rows": draw_key_rows(jax.random.fold_in(key_list[4], 71), 0),
        "value_rows": normal_values(key_list[2], (TOKENS, KV_HEADS * HEAD_DIM), 1.0, 6.0, ((0, 256),)),
        "doc_lengths": uneven_parts(key_list[3], DOCS, TOKENS, SECTION, 2).astype(jnp.int32),
    }


def doc_numbers(doc_lengths, positions):
    starts = jnp.cumsum(doc_lengths) - doc_lengths
    return jnp.sum((positions[:, None] >= starts[None, :]).astype(jnp.int32), axis=1) - 1


def reference(query_rows, key_rows, value_rows, doc_lengths):
    block_rows = min(512, TOKENS)
    window = SECTION
    group_size = HEADS // KV_HEADS
    score_scale = 1.0 / (HEAD_DIM ** 0.5)
    positions = jnp.arange(TOKENS, dtype=jnp.int32)
    doc_all = doc_numbers(doc_lengths, positions)
    key_padded = jnp.concatenate([jnp.zeros((window, KV_HEADS * HEAD_DIM), key_rows.dtype), key_rows], axis=0)
    value_padded = jnp.concatenate([jnp.zeros((window, KV_HEADS * HEAD_DIM), value_rows.dtype), value_rows], axis=0)
    doc_padded = jnp.concatenate([jnp.full((window,), -1, jnp.int32), doc_all], axis=0)

    def one_block(block_index):
        first_row = (block_index * block_rows).astype(jnp.int32)
        queries = lax.dynamic_slice_in_dim(query_rows, first_row, block_rows, 0)
        query_pos = first_row + jnp.arange(block_rows, dtype=jnp.int32)
        query_docs = lax.dynamic_slice_in_dim(doc_all, first_row, block_rows, 0)
        keys_here = lax.dynamic_slice_in_dim(key_padded, first_row, window + block_rows, 0)
        values_here = lax.dynamic_slice_in_dim(value_padded, first_row, window + block_rows, 0)
        key_docs = lax.dynamic_slice_in_dim(doc_padded, first_row, window + block_rows, 0)
        key_pos = first_row - window + jnp.arange(window + block_rows, dtype=jnp.int32)
        allowed = (key_docs[None, :] == query_docs[:, None]) & (key_pos[None, :] <= query_pos[:, None]) & (key_pos[None, :] >= 0)
        query_four = queries.astype(jnp.float32).reshape(block_rows, KV_HEADS, group_size, HEAD_DIM)
        key_three = keys_here.astype(jnp.float32).reshape(window + block_rows, KV_HEADS, HEAD_DIM)
        value_three = values_here.astype(jnp.float32).reshape(window + block_rows, KV_HEADS, HEAD_DIM)
        scores = jnp.einsum("rhgd,phd->hgrp", query_four, key_three) * score_scale
        scores = jnp.where(allowed[None, None], scores, -jnp.inf)
        row_max = jnp.max(scores, axis=-1, keepdims=True)
        weights = jnp.exp(scores - row_max).astype(jnp.bfloat16)
        row_total = jnp.sum(weights.astype(jnp.float32), axis=-1)
        weighted = jnp.einsum("hgrp,phd->hgrd", weights.astype(jnp.float32), value_three)
        result = weighted / row_total[..., None]
        return result.transpose(2, 0, 1, 3).reshape(block_rows, HEADS * HEAD_DIM).astype(jnp.bfloat16)

    blocks = lax.map(one_block, jnp.arange(TOKENS // block_rows, dtype=jnp.int32))
    return blocks.reshape(TOKENS, HEADS * HEAD_DIM)
```

```python
import math

import jax
import jax.numpy as jnp
from jax import lax
from jax.experimental import pallas as pl
from jax.experimental.pallas import tpu as pltpu
from jax.sharding import Mesh
from jax.sharding import PartitionSpec as P

HEAD_DIM = 128
AXES = ("z", "core", "y", "x")
SIDE = 4
BACK = 4
TILE = 512
NEG_FILL = -1e30
EXP_SCALE = math.log2(math.e) / math.sqrt(HEAD_DIM)


def attend(bounds, q_ref, start_ref, *refs):
    pieces, (out_ref, values, top_ref, acc_ref) = refs[: BACK + 1], refs[BACK + 1 :]
    rows = q_ref.shape[1]
    group = rows * SIDE
    heads = q_ref.shape[2] // HEAD_DIM
    per_tile = TILE // rows
    tiles = group // TILE

    for k in range(BACK + 1):
        for b in range(SIDE):
            at = k * tiles + b // per_tile
            values[at, (b % per_tile) * rows : (b % per_tile + 1) * rows, :HEAD_DIM] = pieces[k][b, 1]
    values[:, :, HEAD_DIM:] = jnp.ones((values.shape[0], TILE, HEAD_DIM), jnp.bfloat16)

    def one_block(qb, carry):
        first_row = qb * rows
        low = bounds[0, qb]
        high = bounds[1, qb]
        for h in range(heads):
            top_ref[h] = jnp.full((rows, HEAD_DIM), NEG_FILL, jnp.float32)
            acc_ref[h] = jnp.zeros((rows, 2 * HEAD_DIM), jnp.float32)

        for k in range(BACK + 1):
            piece = pieces[k]

            def one_tile(step, carry, k=k, piece=piece):
                t = tiles - 1 - step
                first_key = t * TILE - k * group

                def work(masked):
                    keys = piece[pl.ds(t * per_tile, per_tile), 0].reshape(TILE, HEAD_DIM)
                    value = values[k * tiles + t]
                    if masked:
                        key_pos = first_key + lax.broadcasted_iota(jnp.int32, (rows, TILE), 1)
                        row_pos = first_row + lax.broadcasted_iota(jnp.int32, (rows, TILE), 0)
                        start = jnp.concatenate([start_ref[qb]] * (TILE // HEAD_DIM), axis=1)
                        allowed = (key_pos >= start) & (key_pos <= row_pos)
                    for h in range(heads):
                        query = q_ref[qb, :, h * HEAD_DIM : (h + 1) * HEAD_DIM]
                        s = lax.dot_general(query, keys, (((1,), (1,)), ((), ())), preferred_element_type=jnp.float32)
                        if masked:
                            s = jnp.where(allowed, s, NEG_FILL)
                        old = top_ref[h]
                        new = jnp.maximum(old, jnp.max(s, axis=1, keepdims=True))
                        top_ref[h] = new
                        factor = jnp.exp2((old - new) * EXP_SCALE)
                        wide = jnp.concatenate([new] * (TILE // HEAD_DIM), axis=1)
                        p = jnp.exp2((s - wide) * EXP_SCALE).astype(jnp.bfloat16)
                        grown = jnp.dot(p, value, preferred_element_type=jnp.float32)
                        acc_ref[h] = acc_ref[h] * jnp.concatenate([factor, factor], axis=1) + grown

                needed = (first_key + TILE > low) & (first_key <= first_row + rows - 1)
                plain = (first_key >= high) & (first_key + TILE - 1 <= first_row)

                @pl.when(needed & plain)
                def _():
                    work(False)

                @pl.when(needed & jnp.logical_not(plain))
                def _():
                    work(True)

                return carry

            lax.fori_loop(0, tiles, one_tile, 0)

        for h in range(heads):
            acc = acc_ref[h]
            out_ref[qb, :, h * HEAD_DIM : (h + 1) * HEAD_DIM] = (acc[:, :HEAD_DIM] / acc[:, HEAD_DIM:]).astype(out_ref.dtype)
        return carry

    lax.fori_loop(0, SIDE, one_block, 0)


def attention(bounds, queries, start, pieces):
    rows = queries.shape[1]
    heads = queries.shape[2] // HEAD_DIM
    tiles = rows * SIDE // TILE
    vmem = pl.BlockSpec(memory_space=pltpu.VMEM)
    return pl.pallas_call(
        attend,
        out_shape=jax.ShapeDtypeStruct(queries.shape, jnp.bfloat16),
        in_specs=[pl.BlockSpec(memory_space=pltpu.SMEM)] + [vmem] * (2 + len(pieces)),
        out_specs=vmem,
        scratch_shapes=[
            pltpu.VMEM(((BACK + 1) * tiles, TILE, 2 * HEAD_DIM), jnp.bfloat16),
            pltpu.VMEM((heads, rows, HEAD_DIM), jnp.float32),
            pltpu.VMEM((heads, rows, 2 * HEAD_DIM), jnp.float32),
        ],
        compiler_params=pltpu.CompilerParams(vmem_limit_bytes=32 * 2**20),
        name="attention",
    )(bounds, queries, start, *pieces)


def document_starts(doc_lengths, positions):
    docs = doc_lengths.shape[0]
    order = jnp.arange(docs)
    starts = jnp.sum(jnp.where(order[None, :] < order[:, None], doc_lengths[None, :], 0), axis=1)
    return jnp.max(jnp.where(starts[None, :] <= positions[:, None], starts[None, :], 0), axis=1)


def shards(query_rows, key_rows, value_rows, doc_lengths):
    rows = query_rows.shape[0]
    group = rows * SIDE
    devices = lax.axis_size(AXES)
    first = (lax.axis_index(AXES) // SIDE) * group

    def by_head(a):
        return a.reshape(rows, SIDE, a.shape[1] // SIDE).transpose(1, 0, 2)

    def exchanged(a):
        return lax.all_to_all(a, "x", 0, 0)

    own = exchanged(jnp.stack([by_head(key_rows), by_head(value_rows)], axis=1))
    pieces = [own]
    for k in range(1, BACK + 1):
        route = [(i, i + SIDE * k) for i in range(devices - SIDE * k)]
        pieces.append(lax.ppermute(own, AXES, route))
    queries = exchanged(by_head(query_rows))

    start = document_starts(doc_lengths, first + jnp.arange(group, dtype=jnp.int32)) - first
    start = start.reshape(SIDE, rows)
    bounds = jnp.stack([start[:, 0], start[:, -1]])
    start = jnp.broadcast_to(start[:, :, None], (SIDE, rows, HEAD_DIM))
    out = exchanged(attention(bounds, queries, start, pieces))
    return out.transpose(1, 0, 2).reshape(query_rows.shape)


def solution(mesh):
    devices = mesh.devices.reshape(-1, 2, SIDE, SIDE)
    split = P(AXES, None)
    return jax.shard_map(
        shards,
        mesh=Mesh(devices, AXES),
        in_specs=(split, split, split, P()),
        out_specs=split,
        check_vma=False,
    )
```

```python
import math

import jax
import jax.numpy as jnp
from jax import lax
from jax.experimental import pallas as pl
from jax.experimental.pallas import tpu as pltpu
from jax.sharding import Mesh
from jax.sharding import PartitionSpec as P

HEAD_DIM = 128
AXES = ("z", "core", "y", "x")
SIDE = 4
BACK = 4
TILE = 512
CHUNK = 256
NEG_FILL = -1e30
EXP_SCALE = math.log2(math.e) / math.sqrt(HEAD_DIM)


def attend(ages, first, last, bounds, q_ref, start_ref, *refs):
    refs = list(refs)
    pieces = [refs.pop(0) for _ in ages]
    before = None if first else (refs.pop(0), refs.pop(0))
    out_ref = refs.pop(0) if last else None
    top_ref, acc_ref, keys, values, score_a, score_b, weight_ref, items = refs
    heads, rows = q_ref.shape[1:3]
    group = rows * SIDE
    stacked = heads * rows
    tiles = group // TILE
    count = len(ages) * tiles

    total = jnp.int32(0)
    items[0] = 0
    for qb in range(SIDE):
        for at in reversed(range(count)):
            first_key = (at % tiles) * TILE - ages[at // tiles] * group
            if first_key <= (qb + 1) * rows - 1:
                items[total] = qb * count + at
                total = total + (first_key + TILE > bounds[0, qb]).astype(jnp.int32)
    items[total] = 0

    for g in range(len(ages)):
        for b in range(SIDE):
            at = g * group + b * rows
            keys[at : at + rows, :] = pieces[g][b, 0]
            values[at : at + rows, :HEAD_DIM] = pieces[g][b, 1]
    values[:, HEAD_DIM:] = jnp.ones((count * TILE, HEAD_DIM), jnp.bfloat16)
    if first:
        top_ref[...] = jnp.full(top_ref.shape, NEG_FILL, jnp.float32)
        acc_ref[...] = jnp.zeros(acc_ref.shape, jnp.float32)
    else:
        top_ref[...] = before[0][...]
        acc_ref[...] = before[1][...]

    def place(item):
        qb = item // count
        at = item - qb * count
        age = jnp.int32(ages[0])
        for g in range(1, len(ages)):
            age = jnp.where(at >= g * tiles, ages[g], age)
        return qb, at, lax.rem(at, tiles) * TILE - age * group

    def score(ref, item):
        qb, at, _ = place(item)
        tile_keys = keys[pl.ds(pl.multiple_of(at * TILE, TILE), TILE)]
        query = q_ref[qb].reshape(stacked, HEAD_DIM)
        ref[...] = lax.dot_general(query, tile_keys, (((1,), (1,)), ((), ())), preferred_element_type=jnp.float32)

    def work(now, later, item, next_item):
        qb, at, first_key = place(item)
        first_row = qb * rows

        @pl.when((first_key < bounds[1, qb]) | (first_key + TILE - 1 > first_row))
        def _():
            key_pos = first_key + lax.broadcasted_iota(jnp.int32, (rows, TILE), 1)
            row_pos = first_row + lax.broadcasted_iota(jnp.int32, (rows, TILE), 0)
            start = jnp.concatenate([start_ref[qb]] * (TILE // HEAD_DIM), axis=1)
            allowed = (key_pos >= start) & (key_pos <= row_pos)
            for h in range(heads):
                part = slice(h * rows, (h + 1) * rows)
                now[part] = jnp.where(allowed, now[part], NEG_FILL)

        score(later, next_item)
        tile_values = values[pl.ds(pl.multiple_of(at * TILE, TILE), TILE)]
        for c in range(0, stacked, CHUNK):
            part = slice(c, c + CHUNK)
            s = now[part]
            old = top_ref[qb, part]
            new = jnp.maximum(old, jnp.max(s, axis=1, keepdims=True))
            top_ref[qb, part] = new
            factor = jnp.exp2((old - new) * EXP_SCALE)
            wide = jnp.concatenate([new] * (TILE // HEAD_DIM), axis=1)
            weight_ref[part] = jnp.exp2((s - wide) * EXP_SCALE).astype(jnp.bfloat16)
            acc_ref[qb, part] = acc_ref[qb, part] * jnp.concatenate([factor, factor], axis=1)
        acc_ref[qb] += jnp.dot(weight_ref[...], tile_values, preferred_element_type=jnp.float32)

    @pl.when(total > 0)
    def _():
        score(score_a, items[0])

    def two(step, carry):
        item, following = items[2 * step], items[2 * step + 1]
        work(score_a, score_b, item, following)

        @pl.when(2 * step + 1 < total)
        def _():
            work(score_b, score_a, following, items[2 * step + 2])

        return carry

    lax.fori_loop(0, (total + 1) // 2, two, 0)

    if last:
        for qb in range(SIDE):
            for h in range(heads):
                acc = acc_ref[qb, h * rows : (h + 1) * rows]
                out_ref[qb, h] = (acc[:, :HEAD_DIM] / acc[:, HEAD_DIM:]).astype(out_ref.dtype)


def attention(ages, bounds, queries, start, pieces, state=(), last=False):
    heads, rows = queries.shape[1:3]
    stacked = heads * rows
    group = rows * SIDE
    window = len(ages) * group
    vmem = pl.BlockSpec(memory_space=pltpu.VMEM)
    held = [
        jax.ShapeDtypeStruct((SIDE, stacked, HEAD_DIM), jnp.float32),
        jax.ShapeDtypeStruct((SIDE, stacked, 2 * HEAD_DIM), jnp.float32),
    ]
    scratch = [
        pltpu.VMEM((window, HEAD_DIM), jnp.bfloat16),
        pltpu.VMEM((window, 2 * HEAD_DIM), jnp.bfloat16),
        pltpu.VMEM((stacked, TILE), jnp.float32),
        pltpu.VMEM((stacked, TILE), jnp.float32),
        pltpu.VMEM((stacked, TILE), jnp.bfloat16),
        pltpu.SMEM((SIDE * window // TILE + 3,), jnp.int32),
    ]
    if last:
        out_shape = jax.ShapeDtypeStruct(queries.shape, jnp.bfloat16)
        scratch = [pltpu.VMEM(a.shape, a.dtype) for a in held] + scratch
    else:
        out_shape = held
    pairs = group * window * heads
    return pl.pallas_call(
        lambda *refs: attend(ages, not state, last, *refs),
        out_shape=out_shape,
        in_specs=[pl.BlockSpec(memory_space=pltpu.SMEM)] + [vmem] * (2 + len(pieces) + len(state)),
        out_specs=vmem if last else [vmem] * 2,
        scratch_shapes=scratch,
        compiler_params=pltpu.CompilerParams(vmem_limit_bytes=40 * 2**20),
        cost_estimate=pl.CostEstimate(flops=pairs * 6 * HEAD_DIM, bytes_accessed=8 * 2**20, transcendentals=pairs),
        name="attention",
    )(bounds, queries, start, *pieces, *state)


def split_heads(*refs):
    *sources, out_ref = refs
    inner = out_ref.shape[1] // len(sources)
    for g in range(out_ref.shape[0]):
        for i, source in enumerate(sources):
            for h in range(inner):
                at = (g * inner + h) * HEAD_DIM
                out_ref[g, i * inner + h] = source[:, at : at + HEAD_DIM]


def join_heads(source, out_ref):
    inner = source.shape[1]
    for g in range(source.shape[0]):
        for h in range(inner):
            at = (g * inner + h) * HEAD_DIM
            out_ref[:, at : at + HEAD_DIM] = source[g, h]


def relaid(kernel, shape, *arrays):
    vmem = pl.BlockSpec(memory_space=pltpu.VMEM)
    return pl.pallas_call(
        kernel,
        out_shape=jax.ShapeDtypeStruct(shape, jnp.bfloat16),
        in_specs=[vmem] * len(arrays),
        out_specs=vmem,
        compiler_params=pltpu.CompilerParams(vmem_limit_bytes=16 * 2**20),
        name=kernel.__name__,
    )(*arrays)


def document_starts(doc_lengths, positions):
    docs = doc_lengths.shape[0]
    order = jnp.arange(docs)
    starts = jnp.sum(jnp.where(order[None, :] < order[:, None], doc_lengths[None, :], 0), axis=1)
    return jnp.max(jnp.where(starts[None, :] <= positions[:, None], starts[None, :], 0), axis=1)


def shards(query_rows, key_rows, value_rows, doc_lengths):
    rows = query_rows.shape[0]
    group = rows * SIDE
    devices = lax.axis_size(AXES)
    first = (lax.axis_index(AXES) // SIDE) * group

    def exchanged(a):
        return lax.all_to_all(a, "x", 0, 0)

    def older(piece, age):
        return lax.ppermute(piece, AXES, [(i, i + SIDE * age) for i in range(devices - SIDE * age)])

    own = exchanged(relaid(split_heads, (SIDE, 2, rows, HEAD_DIM), key_rows, value_rows))
    pieces = {age: older(own, age) for age in (1, 3, 2, 4)}
    queries = exchanged(relaid(split_heads, (SIDE, SIDE, rows, HEAD_DIM), query_rows))

    start = document_starts(doc_lengths, first + jnp.arange(group, dtype=jnp.int32)) - first
    start = start.reshape(SIDE, rows)
    bounds = jnp.stack([start[:, 0], start[:, -1]])
    start = jnp.broadcast_to(start[:, :, None], (SIDE, rows, HEAD_DIM))
    state = attention((3, 1, 0), bounds, queries, start, [pieces[3], pieces[1], own])
    out = attention((4, 2), bounds, queries, start, [pieces[4], pieces[2]], state, last=True)
    return relaid(join_heads, query_rows.shape, exchanged(out))


def solution(mesh):
    devices = mesh.devices.reshape(-1, 2, SIDE, SIDE)
    split = P(AXES, None)
    return jax.shard_map(
        shards,
        mesh=Mesh(devices, AXES),
        in_specs=(split, split, split, P()),
        out_specs=split,
        check_vma=False,
    )
```

```python
import math

import jax
import jax.numpy as jnp
from jax import lax
from jax.experimental import pallas as pl
from jax.experimental.pallas import tpu as pltpu
from jax.sharding import Mesh
from jax.sharding import PartitionSpec as P

HEAD_DIM = 128
AXES = ("z", "core", "y", "x")
SIDE = 4
BACK = 4
TILE = 512
CHUNK = 256
NEG_FILL = -1e30
EXP_SCALE = math.log2(math.e) / math.sqrt(HEAD_DIM)


def attend(ages, first, last, bounds, block, q_ref, start_ref, *refs):
    refs = list(refs)
    blocks = 1 if last else SIDE
    base = block[0] if last else 0
    pieces = [refs.pop(0) for _ in ages]
    before = None if first else (refs.pop(0), refs.pop(0))
    out_ref = refs.pop(0) if last else None
    top_ref, acc_ref, keys, values, score_a, score_b, weight_ref, items = refs
    heads, rows = q_ref.shape[1:3]
    group = rows * SIDE
    stacked = heads * rows
    tiles = group // TILE
    count = len(ages) * tiles

    total = jnp.int32(0)
    items[0] = 0
    for lb in range(blocks):
        for at in reversed(range(count)):
            first_key = (at % tiles) * TILE - ages[at // tiles] * group
            needed = (first_key + TILE > bounds[0, base + lb]) & (first_key < (base + lb + 1) * rows)
            items[total] = lb * count + at
            total = total + needed.astype(jnp.int32)
    items[total] = 0

    for g in range(len(ages)):
        for b in range(SIDE):
            at = g * group + b * rows
            keys[at : at + rows, :] = pieces[g][b, 0]
            values[at : at + rows, :HEAD_DIM] = pieces[g][b, 1]
    values[:, HEAD_DIM:] = jnp.ones((count * TILE, HEAD_DIM), jnp.bfloat16)
    if first:
        top_ref[...] = jnp.full(top_ref.shape, NEG_FILL, jnp.float32)
        acc_ref[...] = jnp.zeros(acc_ref.shape, jnp.float32)
    else:
        for lb in range(blocks):
            top_ref[lb] = before[0][base + lb]
            acc_ref[lb] = before[1][base + lb]

    def place(item):
        lb = item // count
        at = item - lb * count
        age = jnp.int32(ages[0])
        for g in range(1, len(ages)):
            age = jnp.where(at >= g * tiles, ages[g], age)
        return lb, at, lax.rem(at, tiles) * TILE - age * group

    def score(ref, item):
        lb, at, _ = place(item)
        tile_keys = keys[pl.ds(pl.multiple_of(at * TILE, TILE), TILE)]
        query = q_ref[base + lb].reshape(stacked, HEAD_DIM)
        ref[...] = lax.dot_general(query, tile_keys, (((1,), (1,)), ((), ())), preferred_element_type=jnp.float32)

    def work(now, later, item, next_item):
        lb, at, first_key = place(item)
        qb = base + lb
        first_row = qb * rows

        @pl.when((first_key < bounds[1, qb]) | (first_key + TILE - 1 > first_row))
        def _():
            key_pos = first_key + lax.broadcasted_iota(jnp.int32, (rows, TILE), 1)
            row_pos = first_row + lax.broadcasted_iota(jnp.int32, (rows, TILE), 0)
            start = jnp.concatenate([start_ref[qb]] * (TILE // HEAD_DIM), axis=1)
            allowed = (key_pos >= start) & (key_pos <= row_pos)
            for h in range(heads):
                part = slice(h * rows, (h + 1) * rows)
                now[part] = jnp.where(allowed, now[part], NEG_FILL)

        score(later, next_item)
        tile_values = values[pl.ds(pl.multiple_of(at * TILE, TILE), TILE)]
        for c in range(0, stacked, CHUNK):
            part = slice(c, c + CHUNK)
            s = now[part]
            old = top_ref[lb, part]
            new = jnp.maximum(old, jnp.max(s, axis=1, keepdims=True))
            top_ref[lb, part] = new
            factor = jnp.exp2((old - new) * EXP_SCALE)
            wide = jnp.concatenate([new] * (TILE // HEAD_DIM), axis=1)
            weight_ref[part] = jnp.exp2((s - wide) * EXP_SCALE).astype(jnp.bfloat16)
            acc_ref[lb, part] = acc_ref[lb, part] * jnp.concatenate([factor, factor], axis=1)
        acc_ref[lb] += jnp.dot(weight_ref[...], tile_values, preferred_element_type=jnp.float32)

    @pl.when(total > 0)
    def _():
        score(score_a, items[0])

    def two(step, carry):
        item, following = items[2 * step], items[2 * step + 1]
        work(score_a, score_b, item, following)

        @pl.when(2 * step + 1 < total)
        def _():
            work(score_b, score_a, following, items[2 * step + 2])

        return carry

    lax.fori_loop(0, (total + 1) // 2, two, 0)

    if last:
        for h in range(heads):
            acc = acc_ref[0, h * rows : (h + 1) * rows]
            out_ref[h] = (acc[:, :HEAD_DIM] / acc[:, HEAD_DIM:]).astype(out_ref.dtype)


def attention(ages, bounds, block, queries, start, pieces, state=(), last=False):
    heads, rows = queries.shape[1:3]
    stacked = heads * rows
    group = rows * SIDE
    window = len(ages) * group
    blocks = 1 if last else SIDE
    vmem = pl.BlockSpec(memory_space=pltpu.VMEM)
    held = [
        jax.ShapeDtypeStruct((blocks, stacked, HEAD_DIM), jnp.float32),
        jax.ShapeDtypeStruct((blocks, stacked, 2 * HEAD_DIM), jnp.float32),
    ]
    scratch = [
        pltpu.VMEM((window, HEAD_DIM), jnp.bfloat16),
        pltpu.VMEM((window, 2 * HEAD_DIM), jnp.bfloat16),
        pltpu.VMEM((stacked, TILE), jnp.float32),
        pltpu.VMEM((stacked, TILE), jnp.float32),
        pltpu.VMEM((stacked, TILE), jnp.bfloat16),
        pltpu.SMEM((blocks * window // TILE + 3,), jnp.int32),
    ]
    if last:
        out_shape = jax.ShapeDtypeStruct(queries.shape[1:], jnp.bfloat16)
        scratch = [pltpu.VMEM(a.shape, a.dtype) for a in held] + scratch
    else:
        out_shape = held
    pairs = blocks * rows * window * heads
    return pl.pallas_call(
        lambda *refs: attend(ages, not state, last, *refs),
        out_shape=out_shape,
        in_specs=[pl.BlockSpec(memory_space=pltpu.SMEM)] * 2 + [vmem] * (2 + len(pieces) + len(state)),
        out_specs=vmem if last else [vmem] * 2,
        scratch_shapes=scratch,
        compiler_params=pltpu.CompilerParams(vmem_limit_bytes=24 * 2**20),
        cost_estimate=pl.CostEstimate(flops=pairs * 6 * HEAD_DIM, bytes_accessed=8 * 2**20, transcendentals=pairs),
        name="attention",
    )(bounds, block, queries, start, *pieces, *state)


def split_heads(*refs):
    *sources, out_ref = refs
    inner = out_ref.shape[1] // len(sources)
    for g in range(out_ref.shape[0]):
        for i, source in enumerate(sources):
            for h in range(inner):
                at = (g * inner + h) * HEAD_DIM
                out_ref[g, i * inner + h] = source[:, at : at + HEAD_DIM]


def join_heads(place, *refs):
    *sources, out_ref = refs
    for i, source in enumerate(sources):
        for h in range(source.shape[0]):
            at = pl.multiple_of((place[i] * source.shape[0] + h) * HEAD_DIM, HEAD_DIM)
            out_ref[:, pl.ds(at, HEAD_DIM)] = source[h]


def relaid(kernel, shape, *arrays):
    vmem = pl.BlockSpec(memory_space=pltpu.VMEM)
    return pl.pallas_call(
        kernel,
        out_shape=jax.ShapeDtypeStruct(shape, jnp.bfloat16),
        in_specs=[pl.BlockSpec(memory_space=pltpu.SMEM) if a.dtype == jnp.int32 else vmem for a in arrays],
        out_specs=vmem,
        compiler_params=pltpu.CompilerParams(vmem_limit_bytes=16 * 2**20),
        name=kernel.__name__,
    )(*arrays)


def document_starts(doc_lengths, positions):
    docs = doc_lengths.shape[0]
    order = jnp.arange(docs)
    starts = jnp.sum(jnp.where(order[None, :] < order[:, None], doc_lengths[None, :], 0), axis=1)
    return jnp.max(jnp.where(starts[None, :] <= positions[:, None], starts[None, :], 0), axis=1)


def shards(query_rows, key_rows, value_rows, doc_lengths):
    rows = query_rows.shape[0]
    group = rows * SIDE
    devices = lax.axis_size(AXES)
    first = (lax.axis_index(AXES) // SIDE) * group

    def exchanged(a):
        return lax.all_to_all(a, "x", 0, 0)

    def older(piece, age):
        return lax.ppermute(piece, AXES, [(i, i + SIDE * age) for i in range(devices - SIDE * age)])

    own = exchanged(relaid(split_heads, (SIDE, 2, rows, HEAD_DIM), key_rows, value_rows))
    pieces = {age: older(own, age) for age in (4, 1, 3, 2)}
    queries = exchanged(relaid(split_heads, (SIDE, SIDE, rows, HEAD_DIM), query_rows))

    start = document_starts(doc_lengths, first + jnp.arange(group, dtype=jnp.int32)) - first
    start = start.reshape(SIDE, rows)
    bounds = jnp.stack([start[:, 0], start[:, -1]])
    start = jnp.broadcast_to(start[:, :, None], (SIDE, rows, HEAD_DIM))
    here = lax.axis_index("x").astype(jnp.int32)
    zero = jnp.zeros((1,), jnp.int32)
    state = attention((0,), bounds, zero, queries, start, [own])
    state = attention((4, 1), bounds, zero, queries, start, [pieces[4], pieces[1]], state)
    results = {}
    for step in (2, 1, 3, 0):
        block = lax.rem(here + step, SIDE)[None]
        out = attention((3, 2), bounds, block, queries, start, [pieces[3], pieces[2]], state, last=True)
        results[step] = lax.ppermute(out, "x", [(i, (i + step) % SIDE) for i in range(SIDE)]) if step else out
    place = lax.rem(here + SIDE - jnp.arange(SIDE, dtype=jnp.int32), SIDE)
    return relaid(join_heads, query_rows.shape, place, *[results[step] for step in range(SIDE)])


def solution(mesh):
    devices = mesh.devices.reshape(-1, 2, SIDE, SIDE)
    split = P(AXES, None)
    return jax.shard_map(
        shards,
        mesh=Mesh(devices, AXES),
        in_specs=(split, split, split, P()),
        out_specs=split,
        check_vma=False,
    )
```

```python
import math

import jax
import jax.numpy as jnp
from jax import lax
from jax.experimental import pallas as pl
from jax.experimental.pallas import tpu as pltpu
from jax.sharding import Mesh
from jax.sharding import PartitionSpec as P

HEAD_DIM = 128
AXES = ("z", "core", "y", "x")
SIDE = 4
BACK = 4
CHUNK = 256
NEG_FILL = -1e30
EXP_SCALE = math.log2(math.e) / math.sqrt(HEAD_DIM)


def attend(ages, tile, first, last, bounds, which, start_ref, *refs):
    refs = list(refs)
    blocks = SIDE if last is None else 1
    base = 0 if last is None else last
    sources = [refs.pop(0) for _ in range(blocks)]
    pieces = [refs.pop(0) for _ in ages]
    before = None if first else (refs.pop(0), refs.pop(0))
    out_ref = None if last is None else refs.pop(0)
    top_ref, acc_ref, queries, keys, values, score_a, score_b, weight_ref, items = refs
    heads, rows = sources[0].shape[:2]
    group = rows * SIDE
    stacked = heads * rows
    tiles = group // tile
    count = len(ages) * tiles

    total = jnp.int32(0)
    items[0] = 0
    for lb in range(blocks):
        for at in reversed(range(count)):
            first_key = (at % tiles) * tile - ages[at // tiles] * group
            needed = (first_key + tile > bounds[0, which[base + lb]]) & (first_key < (which[base + lb] + 1) * rows)
            items[total] = lb * count + at
            total = total + needed.astype(jnp.int32)
    items[total] = 0

    for lb in range(blocks):
        queries[lb] = sources[lb][...].reshape(stacked, HEAD_DIM)
    for g in range(len(ages)):
        for b in range(SIDE):
            at = pl.multiple_of(g * group + which[b] * rows, rows)
            keys[pl.ds(at, rows), :] = pieces[g][b, 0]
            values[pl.ds(at, rows), :HEAD_DIM] = pieces[g][b, 1]
    values[:, HEAD_DIM:] = jnp.ones((count * tile, HEAD_DIM), jnp.bfloat16)
    if first:
        top_ref[...] = jnp.full(top_ref.shape, NEG_FILL, jnp.float32)
        acc_ref[...] = jnp.zeros(acc_ref.shape, jnp.float32)
    else:
        for lb in range(blocks):
            top_ref[lb] = before[0][base + lb]
            acc_ref[lb] = before[1][base + lb]

    def place(item):
        lb = item // count
        at = item - lb * count
        age = jnp.int32(ages[0])
        for g in range(1, len(ages)):
            age = jnp.where(at >= g * tiles, ages[g], age)
        return lb, at, lax.rem(at, tiles) * tile - age * group

    def score(ref, item):
        lb, at, _ = place(item)
        tile_keys = keys[pl.ds(pl.multiple_of(at * tile, tile), tile)]
        ref[...] = lax.dot_general(queries[lb], tile_keys, (((1,), (1,)), ((), ())), preferred_element_type=jnp.float32)

    def work(now, later, item, next_item):
        lb, at, first_key = place(item)
        qb = which[base + lb]
        first_row = qb * rows

        @pl.when((first_key < bounds[1, qb]) | (first_key + tile - 1 > first_row))
        def _():
            key_pos = first_key + lax.broadcasted_iota(jnp.int32, (rows, tile), 1)
            row_pos = first_row + lax.broadcasted_iota(jnp.int32, (rows, tile), 0)
            start = jnp.concatenate([start_ref[qb]] * (tile // HEAD_DIM), axis=1)
            allowed = (key_pos >= start) & (key_pos <= row_pos)
            for h in range(heads):
                part = slice(h * rows, (h + 1) * rows)
                now[part] = jnp.where(allowed, now[part], NEG_FILL)

        score(later, next_item)
        tile_values = values[pl.ds(pl.multiple_of(at * tile, tile), tile)]
        for c in range(0, stacked, CHUNK):
            part = slice(c, c + CHUNK)
            s = now[part]
            old = top_ref[lb, part]
            new = jnp.maximum(old, jnp.max(s, axis=1, keepdims=True))
            top_ref[lb, part] = new
            factor = jnp.exp2((old - new) * EXP_SCALE)
            wide = jnp.concatenate([new] * (tile // HEAD_DIM), axis=1)
            weight_ref[part] = jnp.exp2((s - wide) * EXP_SCALE).astype(jnp.bfloat16)
            acc_ref[lb, part] = acc_ref[lb, part] * jnp.concatenate([factor, factor], axis=1)
        acc_ref[lb] += jnp.dot(weight_ref[...], tile_values, preferred_element_type=jnp.float32)

    @pl.when(total > 0)
    def _():
        score(score_a, items[0])

    def two(step, carry):
        item, following = items[2 * step], items[2 * step + 1]
        work(score_a, score_b, item, following)

        @pl.when(2 * step + 1 < total)
        def _():
            work(score_b, score_a, following, items[2 * step + 2])

        return carry

    lax.fori_loop(0, (total + 1) // 2, two, 0)

    if last is not None:
        for h in range(heads):
            acc = acc_ref[0, h * rows : (h + 1) * rows]
            out_ref[h] = (acc[:, :HEAD_DIM] / acc[:, HEAD_DIM:]).astype(out_ref.dtype)


def attention(ages, tile, bounds, which, start, queries, pieces, state=(), last=None):
    heads, rows = queries[0].shape[:2]
    stacked = heads * rows
    group = rows * SIDE
    window = len(ages) * group
    blocks = SIDE if last is None else 1
    vmem = pl.BlockSpec(memory_space=pltpu.VMEM)
    held = [
        jax.ShapeDtypeStruct((blocks, stacked, HEAD_DIM), jnp.float32),
        jax.ShapeDtypeStruct((blocks, stacked, 2 * HEAD_DIM), jnp.float32),
    ]
    scratch = [
        pltpu.VMEM((blocks, stacked, HEAD_DIM), jnp.bfloat16),
        pltpu.VMEM((window, HEAD_DIM), jnp.bfloat16),
        pltpu.VMEM((window, 2 * HEAD_DIM), jnp.bfloat16),
        pltpu.VMEM((stacked, tile), jnp.float32),
        pltpu.VMEM((stacked, tile), jnp.float32),
        pltpu.VMEM((stacked, tile), jnp.bfloat16),
        pltpu.SMEM((blocks * window // tile + 3,), jnp.int32),
    ]
    if last is not None:
        out_shape = jax.ShapeDtypeStruct(queries[0].shape, jnp.bfloat16)
        scratch = [pltpu.VMEM(a.shape, a.dtype) for a in held] + scratch
    else:
        out_shape = held
    pairs = blocks * rows * window * heads
    return pl.pallas_call(
        lambda *refs: attend(ages, tile, not state, last, *refs),
        out_shape=out_shape,
        in_specs=[pl.BlockSpec(memory_space=pltpu.SMEM)] * 2 + [vmem] * (1 + blocks + len(pieces) + len(state)),
        out_specs=[vmem] * 2 if last is None else vmem,
        scratch_shapes=scratch,
        compiler_params=pltpu.CompilerParams(vmem_limit_bytes=24 * 2**20),
        cost_estimate=pl.CostEstimate(flops=pairs * 6 * HEAD_DIM, bytes_accessed=8 * 2**20, transcendentals=pairs),
        name="attention",
    )(bounds, which, start, *queries, *pieces, *state)


def split_keys(place, key_ref, value_ref, *outs):
    for i, out_ref in enumerate(outs):
        at = pl.multiple_of(place[i] * HEAD_DIM, HEAD_DIM)
        out_ref[0] = key_ref[:, pl.ds(at, HEAD_DIM)]
        out_ref[1] = value_ref[:, pl.ds(at, HEAD_DIM)]


def stack_blocks(*refs):
    *sources, out_ref = refs
    for i, source in enumerate(sources):
        out_ref[i] = source[...]


def split_queries(place, source, *outs):
    for i, out_ref in enumerate(outs):
        for h in range(SIDE):
            at = pl.multiple_of((place[i] * SIDE + h) * HEAD_DIM, HEAD_DIM)
            out_ref[h] = source[:, pl.ds(at, HEAD_DIM)]


def join_heads(place, *refs):
    *sources, out_ref = refs
    for i, source in enumerate(sources):
        for h in range(source.shape[0]):
            at = pl.multiple_of((place[i] * source.shape[0] + h) * HEAD_DIM, HEAD_DIM)
            out_ref[:, pl.ds(at, HEAD_DIM)] = source[h]


def relaid(kernel, shape, *arrays, copies=None):
    vmem = pl.BlockSpec(memory_space=pltpu.VMEM)
    return pl.pallas_call(
        kernel,
        out_shape=[jax.ShapeDtypeStruct(shape, jnp.bfloat16)] * copies if copies else jax.ShapeDtypeStruct(shape, jnp.bfloat16),
        in_specs=[pl.BlockSpec(memory_space=pltpu.SMEM) if a.dtype == jnp.int32 else vmem for a in arrays],
        out_specs=[vmem] * copies if copies else vmem,
        compiler_params=pltpu.CompilerParams(vmem_limit_bytes=16 * 2**20),
        name=kernel.__name__,
    )(*arrays)


def document_starts(doc_lengths, positions):
    docs = doc_lengths.shape[0]
    order = jnp.arange(docs)
    starts = jnp.sum(jnp.where(order[None, :] < order[:, None], doc_lengths[None, :], 0), axis=1)
    return jnp.max(jnp.where(starts[None, :] <= positions[:, None], starts[None, :], 0), axis=1)


def shards(query_rows, key_rows, value_rows, doc_lengths):
    rows = query_rows.shape[0]
    group = rows * SIDE
    devices = lax.axis_size(AXES)
    first = (lax.axis_index(AXES) // SIDE) * group

    here = lax.axis_index("x").astype(jnp.int32)
    forward = lax.rem(here + jnp.arange(SIDE, dtype=jnp.int32), SIDE)
    which = lax.rem(here + SIDE - jnp.arange(SIDE, dtype=jnp.int32), SIDE)

    def along_x(a, distance):
        return lax.ppermute(a, "x", [(i, (i + distance) % SIDE) for i in range(SIDE)])

    def older(piece, age):
        return lax.ppermute(piece, AXES, [(i, i + SIDE * age) for i in range(devices - SIDE * age)])

    split = relaid(split_keys, (2, rows, HEAD_DIM), forward, key_rows, value_rows, copies=SIDE)
    blocks = [along_x(a, i) if i else a for i, a in enumerate(split)]
    queries = relaid(split_queries, (SIDE, rows, HEAD_DIM), forward, query_rows, copies=SIDE)
    queries = [along_x(a, i) if i else a for i, a in enumerate(queries)]
    own = relaid(stack_blocks, (SIDE, 2, rows, HEAD_DIM), *blocks)
    pieces = {age: older(own, age) for age in (1, 4, 3, 2)}

    start = document_starts(doc_lengths, first + jnp.arange(group, dtype=jnp.int32)) - first
    start = start.reshape(SIDE, rows)
    bounds = jnp.stack([start[:, 0], start[:, -1]])
    start = jnp.broadcast_to(start[:, :, None], (SIDE, rows, HEAD_DIM))
    state = attention((0,), 512, bounds, which, start, queries, [own])
    state = attention((4, 1), 512, bounds, which, start, queries, [pieces[4], pieces[1]], state)
    results = {}
    for i in (2, 1, 3, 0):
        out = attention((3, 2), 1024, bounds, which, start, [queries[i]], [pieces[3], pieces[2]], state, last=i)
        results[i] = along_x(out, -i) if i else out
    return relaid(join_heads, query_rows.shape, forward, *[results[i] for i in range(SIDE)])


def solution(mesh):
    devices = mesh.devices.reshape(-1, 2, SIDE, SIDE)
    split = P(AXES, None)
    return jax.shard_map(
        shards,
        mesh=Mesh(devices, AXES),
        in_specs=(split, split, split, P()),
        out_specs=split,
        check_vma=False,
    )
```

```python
import math

import jax
import jax.numpy as jnp
from jax import lax
from jax.experimental import pallas as pl
from jax.experimental.pallas import tpu as pltpu
from jax.sharding import Mesh
from jax.sharding import PartitionSpec as P

HEAD_DIM = 128
AXES = ("z", "core", "y", "x")
SIDE = 4
BACK = 4
CHUNK = 256
NEG_FILL = -1e30
EXP_SCALE = math.log2(math.e) / math.sqrt(HEAD_DIM)


def attend(ages, tile, first, last, bounds, which, start_ref, *refs):
    refs = list(refs)
    blocks = SIDE if last is None else len(last)
    base = 0 if last is None else last[0]
    sources = [refs.pop(0) for _ in range(blocks)]
    pieces = [refs.pop(0) for _ in ages]
    before = None if first else (refs.pop(0), refs.pop(0))
    outs = [refs.pop(0) for _ in last or ()]
    top_ref, acc_ref, queries, keys, values, score_a, score_b, weight_ref, items = refs
    heads, rows = sources[0].shape[:2]
    group = rows * SIDE
    stacked = heads * rows
    tiles = group // tile
    count = len(ages) * tiles

    total = jnp.int32(0)
    items[0] = 0
    for lb in range(blocks):
        for at in reversed(range(count)):
            first_key = (at % tiles) * tile - ages[at // tiles] * group
            needed = (first_key + tile > bounds[0, which[base + lb]]) & (first_key < (which[base + lb] + 1) * rows)
            items[total] = lb * count + at
            total = total + needed.astype(jnp.int32)
    items[total] = 0

    for lb in range(blocks):
        queries[lb] = sources[lb][...].reshape(stacked, HEAD_DIM)
    for g in range(len(ages)):
        for b in range(SIDE):
            at = pl.multiple_of(g * group + which[b] * rows, rows)
            keys[pl.ds(at, rows), :] = pieces[g][b, 0]
            values[pl.ds(at, rows), :HEAD_DIM] = pieces[g][b, 1]
    values[:, HEAD_DIM:] = jnp.ones((count * tile, HEAD_DIM), jnp.bfloat16)
    if first:
        top_ref[...] = jnp.full(top_ref.shape, NEG_FILL, jnp.float32)
        acc_ref[...] = jnp.zeros(acc_ref.shape, jnp.float32)
    else:
        for lb in range(blocks):
            top_ref[lb] = before[0][base + lb]
            acc_ref[lb] = before[1][base + lb]

    def place(item):
        lb = item // count
        at = item - lb * count
        age = jnp.int32(ages[0])
        for g in range(1, len(ages)):
            age = jnp.where(at >= g * tiles, ages[g], age)
        return lb, at, lax.rem(at, tiles) * tile - age * group

    def score(ref, item):
        lb, at, _ = place(item)
        tile_keys = keys[pl.ds(pl.multiple_of(at * tile, tile), tile)]
        ref[...] = lax.dot_general(queries[lb], tile_keys, (((1,), (1,)), ((), ())), preferred_element_type=jnp.float32)

    def work(now, later, item, next_item):
        lb, at, first_key = place(item)
        qb = which[base + lb]
        first_row = qb * rows

        @pl.when((first_key < bounds[1, qb]) | (first_key + tile - 1 > first_row))
        def _():
            key_pos = first_key + lax.broadcasted_iota(jnp.int32, (rows, tile), 1)
            row_pos = first_row + lax.broadcasted_iota(jnp.int32, (rows, tile), 0)
            start = jnp.concatenate([start_ref[qb]] * (tile // HEAD_DIM), axis=1)
            allowed = (key_pos >= start) & (key_pos <= row_pos)
            for h in range(heads):
                part = slice(h * rows, (h + 1) * rows)
                now[part] = jnp.where(allowed, now[part], NEG_FILL)

        score(later, next_item)
        tile_values = values[pl.ds(pl.multiple_of(at * tile, tile), tile)]
        for c in range(0, stacked, CHUNK):
            part = slice(c, c + CHUNK)
            s = now[part]
            old = top_ref[lb, part]
            new = jnp.maximum(old, jnp.max(s, axis=1, keepdims=True))
            top_ref[lb, part] = new
            factor = jnp.exp2((old - new) * EXP_SCALE)
            wide = jnp.concatenate([new] * (tile // HEAD_DIM), axis=1)
            weight_ref[part] = jnp.exp2((s - wide) * EXP_SCALE).astype(jnp.bfloat16)
            acc_ref[lb, part] = acc_ref[lb, part] * jnp.concatenate([factor, factor], axis=1)
        acc_ref[lb] += jnp.dot(weight_ref[...], tile_values, preferred_element_type=jnp.float32)

    @pl.when(total > 0)
    def _():
        score(score_a, items[0])

    def two(step, carry):
        item, following = items[2 * step], items[2 * step + 1]
        work(score_a, score_b, item, following)

        @pl.when(2 * step + 1 < total)
        def _():
            work(score_b, score_a, following, items[2 * step + 2])

        return carry

    lax.fori_loop(0, (total + 1) // 2, two, 0)

    for lb, out_ref in enumerate(outs):
        for h in range(heads):
            acc = acc_ref[lb, h * rows : (h + 1) * rows]
            out_ref[h] = (acc[:, :HEAD_DIM] / acc[:, HEAD_DIM:]).astype(out_ref.dtype)


def attention(ages, tile, bounds, which, start, queries, pieces, state=(), last=None):
    heads, rows = queries[0].shape[:2]
    stacked = heads * rows
    group = rows * SIDE
    window = len(ages) * group
    blocks = len(queries)
    vmem = pl.BlockSpec(memory_space=pltpu.VMEM)
    held = [
        jax.ShapeDtypeStruct((blocks, stacked, HEAD_DIM), jnp.float32),
        jax.ShapeDtypeStruct((blocks, stacked, 2 * HEAD_DIM), jnp.float32),
    ]
    scratch = [
        pltpu.VMEM((blocks, stacked, HEAD_DIM), jnp.bfloat16),
        pltpu.VMEM((window, HEAD_DIM), jnp.bfloat16),
        pltpu.VMEM((window, 2 * HEAD_DIM), jnp.bfloat16),
        pltpu.VMEM((stacked, tile), jnp.float32),
        pltpu.VMEM((stacked, tile), jnp.float32),
        pltpu.VMEM((stacked, tile), jnp.bfloat16),
        pltpu.SMEM((blocks * window // tile + 3,), jnp.int32),
    ]
    if last is not None:
        out_shape = [jax.ShapeDtypeStruct(a.shape, jnp.bfloat16) for a in queries]
        scratch = [pltpu.VMEM(a.shape, a.dtype) for a in held] + scratch
    else:
        out_shape = held
    pairs = blocks * rows * window * heads
    return pl.pallas_call(
        lambda *refs: attend(ages, tile, not state, last, *refs),
        out_shape=out_shape,
        in_specs=[pl.BlockSpec(memory_space=pltpu.SMEM)] * 2 + [vmem] * (1 + blocks + len(pieces) + len(state)),
        out_specs=[vmem] * len(out_shape),
        scratch_shapes=scratch,
        compiler_params=pltpu.CompilerParams(vmem_limit_bytes=24 * 2**20),
        cost_estimate=pl.CostEstimate(flops=pairs * 6 * HEAD_DIM, bytes_accessed=8 * 2**20, transcendentals=pairs),
        name="attention",
    )(bounds, which, start, *queries, *pieces, *state)


def split_keys(place, key_ref, value_ref, *outs):
    for i, out_ref in enumerate(outs):
        at = pl.multiple_of(place[i] * HEAD_DIM, HEAD_DIM)
        out_ref[0] = key_ref[:, pl.ds(at, HEAD_DIM)]
        out_ref[1] = value_ref[:, pl.ds(at, HEAD_DIM)]


def stack_blocks(*refs):
    *sources, out_ref = refs
    for i, source in enumerate(sources):
        out_ref[i] = source[...]


def split_queries(place, source, *outs):
    for i, out_ref in enumerate(outs):
        for h in range(SIDE):
            at = pl.multiple_of((place[i] * SIDE + h) * HEAD_DIM, HEAD_DIM)
            out_ref[h] = source[:, pl.ds(at, HEAD_DIM)]


def join_heads(place, *refs):
    *sources, out_ref = refs
    for i, source in enumerate(sources):
        for h in range(source.shape[0]):
            at = pl.multiple_of((place[i] * source.shape[0] + h) * HEAD_DIM, HEAD_DIM)
            out_ref[:, pl.ds(at, HEAD_DIM)] = source[h]


def relaid(kernel, shape, *arrays, copies=None):
    vmem = pl.BlockSpec(memory_space=pltpu.VMEM)
    return pl.pallas_call(
        kernel,
        out_shape=[jax.ShapeDtypeStruct(shape, jnp.bfloat16)] * copies if copies else jax.ShapeDtypeStruct(shape, jnp.bfloat16),
        in_specs=[pl.BlockSpec(memory_space=pltpu.SMEM) if a.dtype == jnp.int32 else vmem for a in arrays],
        out_specs=[vmem] * copies if copies else vmem,
        compiler_params=pltpu.CompilerParams(vmem_limit_bytes=16 * 2**20),
        name=kernel.__name__,
    )(*arrays)


def document_starts(doc_lengths, positions):
    docs = doc_lengths.shape[0]
    order = jnp.arange(docs)
    starts = jnp.sum(jnp.where(order[None, :] < order[:, None], doc_lengths[None, :], 0), axis=1)
    return jnp.max(jnp.where(starts[None, :] <= positions[:, None], starts[None, :], 0), axis=1)


def shards(query_rows, key_rows, value_rows, doc_lengths):
    rows = query_rows.shape[0]
    group = rows * SIDE
    devices = lax.axis_size(AXES)
    first = (lax.axis_index(AXES) // SIDE) * group

    here = lax.axis_index("x").astype(jnp.int32)
    forward = lax.rem(here + jnp.arange(SIDE, dtype=jnp.int32), SIDE)
    which = lax.rem(here + SIDE - jnp.arange(SIDE, dtype=jnp.int32), SIDE)

    def along_x(a, distance):
        return lax.ppermute(a, "x", [(i, (i + distance) % SIDE) for i in range(SIDE)])

    def older(piece, age):
        return lax.ppermute(piece, AXES, [(i, i + SIDE * age) for i in range(devices - SIDE * age)])

    split = relaid(split_keys, (2, rows, HEAD_DIM), forward, key_rows, value_rows, copies=SIDE)
    blocks = [along_x(a, i) if i else a for i, a in enumerate(split)]
    blocks[1], query_rows = lax.optimization_barrier((blocks[1], query_rows))
    queries = relaid(split_queries, (SIDE, rows, HEAD_DIM), forward, query_rows, copies=SIDE)
    queries = [along_x(a, i) if i else a for i, a in enumerate(queries)]
    own = relaid(stack_blocks, (SIDE, 2, rows, HEAD_DIM), *blocks)
    pieces = {age: older(own, age) for age in (1, 4, 3)}

    start = document_starts(doc_lengths, first + jnp.arange(group, dtype=jnp.int32)) - first
    start = start.reshape(SIDE, rows)
    bounds = jnp.stack([start[:, 0], start[:, -1]])
    start = jnp.broadcast_to(start[:, :, None], (SIDE, rows, HEAD_DIM))
    state = attention((0,), 512, bounds, which, start, queries, [own])
    later, state = lax.optimization_barrier((own, state))
    pieces[2] = older(later, 2)
    state = attention((4, 1), 512, bounds, which, start, queries, [pieces[4], pieces[1]], state)
    results = {}
    for group in ((2, 3), (1,), (0,)):
        sources = [queries[i] for i in group]
        outs = attention((3, 2), 1024, bounds, which, start, sources, [pieces[3], pieces[2]], state, last=group)
        results |= {i: along_x(out, -i) if i else out for i, out in zip(group, outs)}
    return relaid(join_heads, query_rows.shape, forward, *[results[i] for i in range(SIDE)])


def solution(mesh):
    devices = mesh.devices.reshape(-1, 2, SIDE, SIDE)
    split = P(AXES, None)
    return jax.shard_map(
        shards,
        mesh=Mesh(devices, AXES),
        in_specs=(split, split, split, P()),
        out_specs=split,
        check_vma=False,
    )
```

```python
import math

import jax
import jax.numpy as jnp
from jax import lax
from jax.experimental import pallas as pl
from jax.experimental.pallas import tpu as pltpu
from jax.sharding import Mesh
from jax.sharding import PartitionSpec as P

HEAD_DIM = 128
AXES = ("z", "core", "y", "x")
SIDE = 4
BACK = 4
CHUNK = 256
NEG_FILL = -1e30
EXP_SCALE = math.log2(math.e) / math.sqrt(HEAD_DIM)


def attend(ages, tile, first, last, bounds, which, start_ref, *refs):
    refs = list(refs)
    blocks = SIDE if last is None else len(last)
    base = 0 if last is None else last[0]
    sources = [refs.pop(0) for _ in range(blocks)]
    pieces = [refs.pop(0) for _ in ages]
    before = None if first else (refs.pop(0), refs.pop(0))
    outs = [refs.pop(0) for _ in last or ()]
    top_ref, acc_ref, queries, keys, values, score_a, score_b, weight_ref, items = refs
    heads, rows = sources[0].shape[:2]
    group = rows * SIDE
    stacked = heads * rows
    tiles = group // tile
    count = len(ages) * tiles

    total = jnp.int32(0)
    items[0] = 0
    for lb in range(blocks):
        for at in reversed(range(count)):
            first_key = (at % tiles) * tile - ages[at // tiles] * group
            needed = (first_key + tile > bounds[0, which[base + lb]]) & (first_key < (which[base + lb] + 1) * rows)
            items[total] = lb * count + at
            total = total + needed.astype(jnp.int32)
    items[total] = 0

    for lb in range(blocks):
        queries[lb] = sources[lb][...].reshape(stacked, HEAD_DIM)
    for g in range(len(ages)):
        for b in range(SIDE):
            at = pl.multiple_of(g * group + which[b] * rows, rows)
            keys[pl.ds(at, rows), :] = pieces[g][b, 0]
            values[pl.ds(at, rows), :HEAD_DIM] = pieces[g][b, 1]
    values[:, HEAD_DIM:] = jnp.ones((count * tile, HEAD_DIM), jnp.bfloat16)
    if first:
        top_ref[...] = jnp.full(top_ref.shape, NEG_FILL, jnp.float32)
        acc_ref[...] = jnp.zeros(acc_ref.shape, jnp.float32)
    else:
        for lb in range(blocks):
            top_ref[lb] = before[0][base + lb]
            acc_ref[lb] = before[1][base + lb]

    def place(item):
        lb = item // count
        at = item - lb * count
        age = jnp.int32(ages[0])
        for g in range(1, len(ages)):
            age = jnp.where(at >= g * tiles, ages[g], age)
        return lb, at, lax.rem(at, tiles) * tile - age * group

    def score(ref, item):
        lb, at, _ = place(item)
        tile_keys = keys[pl.ds(pl.multiple_of(at * tile, tile), tile)]
        ref[...] = lax.dot_general(queries[lb], tile_keys, (((1,), (1,)), ((), ())), preferred_element_type=jnp.float32)

    def work(now, later, item, next_item):
        lb, at, first_key = place(item)
        qb = which[base + lb]
        first_row = qb * rows

        @pl.when((first_key < bounds[1, qb]) | (first_key + tile - 1 > first_row))
        def _():
            key_pos = first_key + lax.broadcasted_iota(jnp.int32, (rows, tile), 1)
            row_pos = first_row + lax.broadcasted_iota(jnp.int32, (rows, tile), 0)
            start = jnp.concatenate([start_ref[qb]] * (tile // HEAD_DIM), axis=1)
            allowed = (key_pos >= start) & (key_pos <= row_pos)
            for h in range(heads):
                part = slice(h * rows, (h + 1) * rows)
                now[part] = jnp.where(allowed, now[part], NEG_FILL)

        score(later, next_item)
        tile_values = values[pl.ds(pl.multiple_of(at * tile, tile), tile)]
        for c in range(0, stacked, CHUNK):
            part = slice(c, c + CHUNK)
            s = now[part]
            old = top_ref[lb, part]
            new = jnp.maximum(old, jnp.max(s, axis=1, keepdims=True))
            top_ref[lb, part] = new
            factor = jnp.exp2((old - new) * EXP_SCALE)
            wide = jnp.concatenate([new] * (tile // HEAD_DIM), axis=1)
            weight_ref[part] = jnp.exp2((s - wide) * EXP_SCALE).astype(jnp.bfloat16)
            acc_ref[lb, part] = acc_ref[lb, part] * jnp.concatenate([factor, factor], axis=1)
        acc_ref[lb] += jnp.dot(weight_ref[...], tile_values, preferred_element_type=jnp.float32)

    @pl.when(total > 0)
    def _():
        score(score_a, items[0])

    def two(step, carry):
        item, following = items[2 * step], items[2 * step + 1]
        work(score_a, score_b, item, following)

        @pl.when(2 * step + 1 < total)
        def _():
            work(score_b, score_a, following, items[2 * step + 2])

        return carry

    lax.fori_loop(0, (total + 1) // 2, two, 0)

    for lb, out_ref in enumerate(outs):
        for h in range(heads):
            acc = acc_ref[lb, h * rows : (h + 1) * rows]
            out_ref[h] = (acc[:, :HEAD_DIM] / acc[:, HEAD_DIM:]).astype(out_ref.dtype)


def attention(ages, tile, bounds, which, start, queries, pieces, state=(), last=None):
    heads, rows = queries[0].shape[:2]
    stacked = heads * rows
    group = rows * SIDE
    window = len(ages) * group
    blocks = len(queries)
    vmem = pl.BlockSpec(memory_space=pltpu.VMEM)
    held = [
        jax.ShapeDtypeStruct((blocks, stacked, HEAD_DIM), jnp.float32),
        jax.ShapeDtypeStruct((blocks, stacked, 2 * HEAD_DIM), jnp.float32),
    ]
    scratch = [
        pltpu.VMEM((blocks, stacked, HEAD_DIM), jnp.bfloat16),
        pltpu.VMEM((window, HEAD_DIM), jnp.bfloat16),
        pltpu.VMEM((window, 2 * HEAD_DIM), jnp.bfloat16),
        pltpu.VMEM((stacked, tile), jnp.float32),
        pltpu.VMEM((stacked, tile), jnp.float32),
        pltpu.VMEM((stacked, tile), jnp.bfloat16),
        pltpu.SMEM((blocks * window // tile + 3,), jnp.int32),
    ]
    if last is not None:
        out_shape = [jax.ShapeDtypeStruct(a.shape, jnp.bfloat16) for a in queries]
        scratch = [pltpu.VMEM(a.shape, a.dtype) for a in held] + scratch
    else:
        out_shape = held
    pairs = blocks * rows * window * heads
    return pl.pallas_call(
        lambda *refs: attend(ages, tile, not state, last, *refs),
        out_shape=out_shape,
        in_specs=[pl.BlockSpec(memory_space=pltpu.SMEM)] * 2 + [vmem] * (1 + blocks + len(pieces) + len(state)),
        out_specs=[vmem] * len(out_shape),
        scratch_shapes=scratch,
        compiler_params=pltpu.CompilerParams(vmem_limit_bytes=24 * 2**20),
        cost_estimate=pl.CostEstimate(flops=pairs * 6 * HEAD_DIM, bytes_accessed=8 * 2**20, transcendentals=pairs),
        name="attention",
    )(bounds, which, start, *queries, *pieces, *state)


def split_keys(place, key_source, value_source, *refs):
    *outs, key_ref, value_ref, key_sem, value_sem = refs
    key_copy = pltpu.make_async_copy(key_source, key_ref, key_sem)
    value_copy = pltpu.make_async_copy(value_source, value_ref, value_sem)
    key_copy.start()
    value_copy.start()
    key_copy.wait()
    value_copy.wait()
    for i, out_ref in enumerate(outs):
        at = pl.multiple_of(place[i] * HEAD_DIM, HEAD_DIM)
        out_ref[0] = key_ref[:, pl.ds(at, HEAD_DIM)]
        out_ref[1] = value_ref[:, pl.ds(at, HEAD_DIM)]


def stack_blocks(*refs):
    *sources, out_ref = refs
    for i, source in enumerate(sources):
        out_ref[i] = source[...]


def split_queries(place, source, *outs):
    for i, out_ref in enumerate(outs):
        for h in range(SIDE):
            at = pl.multiple_of((place[i] * SIDE + h) * HEAD_DIM, HEAD_DIM)
            out_ref[h] = source[:, pl.ds(at, HEAD_DIM)]


def join_heads(place, *refs):
    *sources, out_ref = refs
    for i, source in enumerate(sources):
        for h in range(source.shape[0]):
            at = pl.multiple_of((place[i] * source.shape[0] + h) * HEAD_DIM, HEAD_DIM)
            out_ref[:, pl.ds(at, HEAD_DIM)] = source[h]


def relaid(kernel, shape, *arrays, copies=None):
    vmem = pl.BlockSpec(memory_space=pltpu.VMEM)
    return pl.pallas_call(
        kernel,
        out_shape=[jax.ShapeDtypeStruct(shape, jnp.bfloat16)] * copies if copies else jax.ShapeDtypeStruct(shape, jnp.bfloat16),
        in_specs=[pl.BlockSpec(memory_space=pltpu.SMEM) if a.dtype == jnp.int32 else vmem for a in arrays],
        out_specs=[vmem] * copies if copies else vmem,
        compiler_params=pltpu.CompilerParams(vmem_limit_bytes=16 * 2**20),
        name=kernel.__name__,
    )(*arrays)


def document_starts(doc_lengths, positions):
    docs = doc_lengths.shape[0]
    order = jnp.arange(docs)
    starts = jnp.sum(jnp.where(order[None, :] < order[:, None], doc_lengths[None, :], 0), axis=1)
    return jnp.max(jnp.where(starts[None, :] <= positions[:, None], starts[None, :], 0), axis=1)


def shards(query_rows, key_rows, value_rows, doc_lengths):
    rows = query_rows.shape[0]
    group = rows * SIDE
    devices = lax.axis_size(AXES)
    first = (lax.axis_index(AXES) // SIDE) * group

    here = lax.axis_index("x").astype(jnp.int32)
    forward = lax.rem(here + jnp.arange(SIDE, dtype=jnp.int32), SIDE)
    which = lax.rem(here + SIDE - jnp.arange(SIDE, dtype=jnp.int32), SIDE)

    def along_x(a, distance):
        return lax.ppermute(a, "x", [(i, (i + distance) % SIDE) for i in range(SIDE)])

    def older(piece, age):
        return lax.ppermute(piece, AXES, [(i, i + SIDE * age) for i in range(devices - SIDE * age)])

    vmem = pl.BlockSpec(memory_space=pltpu.VMEM)
    held = pltpu.VMEM(key_rows.shape, jnp.bfloat16)
    split = pl.pallas_call(
        split_keys,
        out_shape=[jax.ShapeDtypeStruct((2, rows, HEAD_DIM), jnp.bfloat16)] * SIDE,
        in_specs=[pl.BlockSpec(memory_space=pltpu.SMEM)] + [pl.BlockSpec(memory_space=pltpu.HBM)] * 2,
        out_specs=[vmem] * SIDE,
        scratch_shapes=[held, held, pltpu.SemaphoreType.DMA, pltpu.SemaphoreType.DMA],
        compiler_params=pltpu.CompilerParams(vmem_limit_bytes=16 * 2**20),
        name="split_keys",
    )(forward, key_rows, value_rows)
    blocks = [along_x(a, i) if i else a for i, a in enumerate(split)]
    blocks[1], query_rows = lax.optimization_barrier((blocks[1], query_rows))
    queries = relaid(split_queries, (SIDE, rows, HEAD_DIM), forward, query_rows, copies=SIDE)
    queries = [along_x(a, i) if i else a for i, a in enumerate(queries)]
    own = relaid(stack_blocks, (SIDE, 2, rows, HEAD_DIM), *blocks)
    pieces = {age: older(own, age) for age in (1, 4, 3)}

    start = document_starts(doc_lengths, first + jnp.arange(group, dtype=jnp.int32)) - first
    start = start.reshape(SIDE, rows)
    bounds = jnp.stack([start[:, 0], start[:, -1]])
    start = jnp.broadcast_to(start[:, :, None], (SIDE, rows, HEAD_DIM))
    state = attention((0,), 512, bounds, which, start, queries, [own])
    later, state = lax.optimization_barrier((own, state))
    pieces[2] = older(later, 2)
    state = attention((4, 1), 512, bounds, which, start, queries, [pieces[4], pieces[1]], state)
    results = {}
    for group in ((2, 3), (1,), (0,)):
        sources = [queries[i] for i in group]
        outs = attention((3, 2), 1024, bounds, which, start, sources, [pieces[3], pieces[2]], state, last=group)
        results |= {i: along_x(out, -i) if i else out for i, out in zip(group, outs)}
    return relaid(join_heads, query_rows.shape, forward, *[results[i] for i in range(SIDE)])


def solution(mesh):
    devices = mesh.devices.reshape(-1, 2, SIDE, SIDE)
    split = P(AXES, None)
    return jax.shard_map(
        shards,
        mesh=Mesh(devices, AXES),
        in_specs=(split, split, split, P()),
        out_specs=split,
        check_vma=False,
    )
```
